32 devices in a mesh: seq: 4 (over y, x), head: 8 (over z, core).
Axes of the slice: x: 2, y: 2, z: 4, core: 2. Of those that a mesh axis runs over, the one named last changes fastest.
Arguments:
- query_rows: bfloat16 [4, 2048, 8192], P(None, 'seq', 'head'), may hold values from -6 to 6
- key_rows: bfloat16 [4, 2048, 8192], P(None, 'seq', 'head'), may hold values from -6 to 6
- value_rows: bfloat16 [4, 2048, 8192], P(None, 'seq', 'head'), may hold values from -6 to 6
- prior_state: float32 [4, 64, 128, 128], P(None, 'head'), may hold values from -256 to 256
- tree_query: bfloat16 [4, 256, 8192], P(None, 'seq', 'head'), may hold values from -6 to 6
- tree_key: bfloat16 [4, 256, 8192], P(None, 'seq', 'head'), may hold values from -6 to 6
- tree_value: bfloat16 [4, 256, 8192], P(None, 'seq', 'head'), may hold values from -12 to 12
- parents: int32 [4, 256], replicated, may hold values from 0 to 254, as said below
- out_weight: bfloat16 [8192, 8192], P('head', 'seq'), may hold values from -0.0625 to 0.0625
Outputs:
- prefill_out: bfloat16 [4, 2048, 8192], P(None, 'seq', 'head')
- verified: bfloat16 [1024, 8192], P('head', 'seq')
The draws below stay inside these ranges and needn't reach their ends.
Inputs may be any that keep to these rules, and one draw needn't show every extreme that they name: parents[r, 0] is 0; for every node n >= 1, parents[r, n] lies between n - 4 and n - 1 and is at least 0.
All inputs are finite; a program needn't handle non-finite values.
Results may differ from the reference program's by a relative error of at most 0.023.
Values may be sent and summed in bfloat16 or wider, within the bound.
A program may use at most 128 MiB of HBM per device.

```python
import jax
import jax.numpy as jnp
from jax import lax

D = 8192
H = 64
DH = 128
R = 4
TOK_DEV = 512
NODES = 256
HD = 8192
WINDOW = 2048
N_SEQ = 4


def draw_parents(key, part):
    backward = jax.random.randint(jax.random.fold_in(key, 11), (R, NODES), 1, 5)
    node_ids = jnp.arange(NODES).astype(jnp.int32)
    return jnp.maximum(node_ids[None, :] - backward, 0).astype(jnp.int32)


def steps_of(rng, dims, cuts, least, largest):
    factor_of = 1.0
    for axis_at, shards_of in cuts:
        steps = jax.random.uniform(jax.random.fold_in(jax.random.fold_in(rng, 6), axis_at), (shards_of,), jnp.float32, least / len(cuts), largest / len(cuts))
        factor_of = factor_of * jnp.repeat(jnp.exp(steps), dims[axis_at] // shards_of).reshape((-1,) + (1,) * (len(dims) - 1 - axis_at))
    return factor_of


def noise(own_key, shape, spread, most, cuts=(), dtype=jnp.bfloat16):
    drawn = jax.random.normal(own_key, shape, jnp.float32) * spread
    if len(cuts) > 0:
        drawn = steps_of(own_key, shape, cuts, -0.22, 0.18) * drawn
    return jnp.clip(drawn, min=-most, max=most).astype(dtype)


def setup_inputs(seed: int = 0) -> dict:
    key_of = jax.random.split(jax.random.key(seed), 10)
    return {
        "query_rows": noise(key_of[0], (R, WINDOW, HD), 1.0, 6.0, ((1, 4), (2, 8))),
        "key_rows": noise(key_of[1], (R, WINDOW, HD), 1.0, 6.0, ((1, 4), (2, 8))),
        "value_rows": noise(key_of[2], (R, WINDOW, HD), 1.0, 6.0, ((1, 4), (2, 8))),
        "prior_state": noise(key_of[3], (R, H, DH, DH), ((TOK_DEV * N_SEQ) ** 0.5), 256.0, ((1, 8),), jnp.float32),
        "tree_query": noise(key_of[4], (R, NODES, HD), 1.0, 6.0, ((1, 4), (2, 8))),
        "tree_key": noise(key_of[5], (R, NODES, HD), 1.0, 6.0, ((1, 4), (2, 8))),
        "tree_value": noise(key_of[6], (R, NODES, HD), 2.0, 12.0, ((1, 4), (2, 8))),
        "parents": draw_parents(jax.random.fold_in(key_of[9], 71), 0),
        "out_weight": noise(key_of[8], (HD, D), HD ** -0.5, 0.0625, ((0, 8), (1, 4))),
    }


epsilon = 1e-05

def head_norm(field):
    return field * lax.rsqrt(lax.optimization_barrier(jnp.mean(field * field, axis=-1, keepdims=True)) + epsilon)

def held_bf16(field):
    return lax.optimization_barrier(field.astype(jnp.bfloat16)).astype(jnp.float32)

def reference(query_rows, key_rows, value_rows, prior_state, tree_query, tree_key, tree_value, parents, out_weight):
    block = min(512, TOK_DEV)
    window = TOK_DEV * N_SEQ
    blocks = window // block
    highest = lax.Precision.HIGHEST

    def split(field):
        return field.reshape(R, blocks, block, H, DH).transpose(1, 0, 2, 3, 4)
    causal = jnp.arange(block)[:, None] >= jnp.arange(block)[None, :]

    def advance(state, inputs):
        q_block, k_block, v_block = inputs
        q_float = q_block.astype(jnp.float32)
        k_float = k_block.astype(jnp.float32)
        v_float = v_block.astype(jnp.float32)
        context = jnp.einsum('rbhd,rhde->rbhe', q_float, held_bf16(state), precision=highest)
        scores = jnp.einsum('rbhd,rchd->rhbc', q_float, k_float, precision=highest)
        weights = held_bf16(jnp.where(causal[None, None], scores, 0.0))
        inner = jnp.einsum('rhbc,rchd->rbhd', weights, v_float, precision=highest)
        block_out = head_norm(context + inner).astype(jnp.bfloat16)
        state = state + jnp.einsum('rchd,rche->rhde', k_float, v_float, precision=highest)
        return (state, block_out)
    total, outputs = lax.scan(advance, prior_state, (split(query_rows), split(key_rows), split(value_rows)))
    prefill_out = outputs.transpose(1, 0, 2, 3, 4).reshape(R, window, H * DH)
    node_ids = jnp.arange(NODES).astype(jnp.int32)
    links = (parents[:, :, None] == node_ids[None, None, :]) & (node_ids[None, :, None] >= 1)
    itself = (node_ids[:, None] == node_ids[None, :])[None]
    reach = (links | itself).astype(jnp.bfloat16)
    for level in range((NODES - 1).bit_length()):
        square = jnp.einsum('pij,pjk->pik', reach.astype(jnp.float32), reach.astype(jnp.float32), precision=highest)
        reach = jnp.minimum(square, 1.0).astype(jnp.bfloat16)
    tree_q = tree_query.reshape(R, NODES, H, DH).astype(jnp.float32)
    tree_k = tree_key.reshape(R, NODES, H, DH).astype(jnp.float32)
    tree_v = tree_value.reshape(R, NODES, H, DH).astype(jnp.float32)
    tree_context = jnp.einsum('rkhd,rhde->rkhe', tree_q, held_bf16(total), precision=highest)
    tree_scores = jnp.einsum('rkhd,rmhd->rhkm', tree_q, tree_k, precision=highest)
    tree_weights = held_bf16(jnp.where(reach[:, None] > 0, tree_scores, 0.0))
    tree_mixed = jnp.einsum('rhkm,rmhd->rkhd', tree_weights, tree_v, precision=highest)
    node_out = head_norm(tree_context + tree_mixed).astype(jnp.bfloat16).reshape(R * NODES, H * DH)
    verified = jnp.dot(node_out, out_weight, preferred_element_type=jnp.float32).astype(jnp.bfloat16)
    return (prefill_out, verified)
```

```python
import functools

import jax
import jax.numpy as jnp
from jax import lax
from jax.experimental import pallas as pl
from jax.experimental.pallas import tpu as pltpu
from jax.sharding import PartitionSpec as P

DH = 128
epsilon = 1e-05
VMEM_BYTES = 40 * 1024 * 1024


def head_norm(field):
    return field * lax.rsqrt(jnp.mean(field * field, axis=-1, keepdims=True) + epsilon)


def dot(a, b, over_a=1, over_b=0):
    return lax.dot_general(
        a, b, (((over_a,), (over_b,)), ((), ())), preferred_element_type=jnp.float32
    )


def columns(h):
    return slice(h * DH, (h + 1) * DH)


def kv_kernel(k_ref, v_ref, out_ref):
    for h in range(out_ref.shape[1]):
        out_ref[0, h] = dot(k_ref[0, :, columns(h)], v_ref[0, :, columns(h)], 0, 0).astype(
            jnp.bfloat16
        )


def reach_kernel(parents_ref, out_ref):
    nodes = out_ref.shape[0]
    row = lax.broadcasted_iota(jnp.int32, (nodes, nodes), 0)
    column = lax.broadcasted_iota(jnp.int32, (nodes, nodes), 1)
    links = (parents_ref[...] == column) & (row >= 1)
    reach = jnp.where(links | (row == column), 1.0, 0.0).astype(jnp.bfloat16)
    for level in range((nodes - 1).bit_length()):
        reach = jnp.minimum(dot(reach, reach), 1.0).astype(jnp.bfloat16)
    out_ref[...] = reach


def tree_kernel(pieces, qkv_ref, parts_ref, prior_ref, reach_ref, out_ref, base_ref):
    wide = pieces * DH
    reached = reach_ref[...] > 0
    for p in range(pieces):
        state = prior_ref[p]
        for s in range(parts_ref.shape[0]):
            base_ref[s, p] = state.astype(jnp.bfloat16)
            state = state + parts_ref[s, p].astype(jnp.float32)
        q = qkv_ref[:, p * DH : (p + 1) * DH]
        k = qkv_ref[:, wide + p * DH : wide + (p + 1) * DH]
        v = qkv_ref[:, 2 * wide + p * DH : 2 * wide + (p + 1) * DH]
        weights = jnp.where(reached, dot(q, k, 1, 1), 0.0).astype(jnp.bfloat16)
        raw = dot(q, state.astype(jnp.bfloat16)) + dot(weights, v)
        out_ref[:, columns(p)] = head_norm(raw).astype(jnp.bfloat16)


def prefill_kernel(heads, q_ref, k_ref, v_ref, base_ref, out_ref):
    tokens = q_ref.shape[1]
    rows = min(256, tokens)
    row = lax.broadcasted_iota(jnp.int32, (rows, rows), 0)
    column = lax.broadcasted_iota(jnp.int32, (rows, rows), 1)
    causal = row >= column
    for h in range(heads):
        for at in range(0, tokens, rows):
            q = q_ref[0, at : at + rows, columns(h)]
            raw = dot(q, base_ref[0, h])
            here = dot(q, k_ref[0, at : at + rows, columns(h)], 1, 1)
            here = jnp.where(causal, here, 0.0).astype(jnp.bfloat16)
            raw = raw + dot(here, v_ref[0, at : at + rows, columns(h)])
            if at:
                past = dot(q, k_ref[0, :at, columns(h)], 1, 1).astype(jnp.bfloat16)
                raw = raw + dot(past, v_ref[0, :at, columns(h)])
            out_ref[0, at : at + rows, columns(h)] = head_norm(raw).astype(jnp.bfloat16)


def on_device(
    query_rows,
    key_rows,
    value_rows,
    prior_state,
    tree_query,
    tree_key,
    tree_value,
    parents,
    out_weight,
):
    requests, tokens, width = query_rows.shape
    heads = width // DH
    assert tokens <= 512
    seq_index = lax.axis_index("seq")
    seq_count = lax.axis_size("seq")
    pieces = requests * heads // seq_count
    groups = heads // pieces
    assert groups * pieces == heads
    nodes_here = tree_query.shape[1]
    nodes = parents.shape[1]
    wide = pieces * DH
    params = pltpu.CompilerParams(vmem_limit_bytes=VMEM_BYTES)

    def to_owners(field):
        field = field.reshape(requests, nodes_here, groups, wide)
        return field.transpose(0, 2, 1, 3).reshape(seq_count, nodes_here, wide)

    packed = jnp.concatenate([to_owners(f) for f in (tree_query, tree_key, tree_value)], axis=2)
    owner_qkv = lax.all_to_all(packed, "seq", split_axis=0, concat_axis=0, tiled=True)
    owner_qkv = owner_qkv.reshape(nodes, 3 * wide)

    rows_spec = pl.BlockSpec((1, tokens, width), lambda r: (r, 0, 0))
    block_kv = pl.pallas_call(
        kv_kernel,
        grid=(requests,),
        in_specs=[rows_spec, rows_spec],
        out_specs=pl.BlockSpec((1, heads, DH, DH), lambda r: (r, 0, 0, 0)),
        out_shape=jax.ShapeDtypeStruct((requests, heads, DH, DH), jnp.bfloat16),
        compiler_params=params,
        cost_estimate=pl.CostEstimate(
            flops=2 * requests * tokens * width * DH,
            bytes_accessed=4 * requests * tokens * width,
            transcendentals=0,
        ),
    )(key_rows, value_rows)
    parts = lax.all_to_all(
        block_kv.reshape(seq_count, pieces, DH, DH), "seq", split_axis=0, concat_axis=0, tiled=True
    )

    own_parents = lax.dynamic_slice_in_dim(parents, seq_index // groups, 1, 0).reshape(nodes, 1)
    reach = pl.pallas_call(
        reach_kernel,
        out_shape=jax.ShapeDtypeStruct((nodes, nodes), jnp.bfloat16),
        compiler_params=params,
        cost_estimate=pl.CostEstimate(
            flops=16 * nodes**3, bytes_accessed=4 * nodes * nodes, transcendentals=0
        ),
    )(own_parents)
    flat_prior = prior_state.reshape(requests * heads, DH, DH)
    owned_prior = lax.dynamic_slice_in_dim(flat_prior, seq_index * pieces, pieces, 0)
    node_out, base = pl.pallas_call(
        functools.partial(tree_kernel, pieces),
        out_shape=(
            jax.ShapeDtypeStruct((nodes, wide), jnp.bfloat16),
            jax.ShapeDtypeStruct((seq_count, pieces, DH, DH), jnp.bfloat16),
        ),
        compiler_params=params,
        cost_estimate=pl.CostEstimate(
            flops=4 * pieces * nodes * nodes * DH,
            bytes_accessed=8 * nodes * wide + 8 * seq_count * pieces * DH * DH,
            transcendentals=0,
        ),
    )(owner_qkv, parts, owned_prior, reach)

    gathered = lax.all_gather(node_out, "seq", axis=0, tiled=True)
    merged = (
        gathered.reshape(requests, groups, nodes, wide)
        .transpose(0, 2, 1, 3)
        .reshape(requests * nodes, width)
    )
    verified = lax.psum_scatter(
        jnp.dot(merged, out_weight, preferred_element_type=jnp.float32).astype(jnp.bfloat16),
        "head",
        scatter_dimension=0,
        tiled=True,
    )

    base = lax.all_to_all(base, "seq", split_axis=0, concat_axis=0, tiled=True)
    base = base.reshape(requests, heads, DH, DH)
    step = min(4, heads)
    step_spec = pl.BlockSpec((1, tokens, step * DH), lambda r, h: (r, 0, h))
    prefill_out = pl.pallas_call(
        functools.partial(prefill_kernel, step),
        grid=(requests, heads // step),
        in_specs=[
            step_spec,
            step_spec,
            step_spec,
            pl.BlockSpec((1, step, DH, DH), lambda r, h: (r, h, 0, 0)),
        ],
        out_specs=step_spec,
        out_shape=jax.ShapeDtypeStruct((requests, tokens, width), jnp.bfloat16),
        compiler_params=params,
        cost_estimate=pl.CostEstimate(
            flops=4 * requests * tokens * tokens * width,
            bytes_accessed=8 * requests * tokens * width,
            transcendentals=0,
        ),
    )(query_rows, key_rows, value_rows, base)
    return (prefill_out, verified)


def solution(mesh):
    placed = (
        P(None, "seq", "head"),
        P(None, "seq", "head"),
        P(None, "seq", "head"),
        P(None, "head", None, None),
        P(None, "seq", "head"),
        P(None, "seq", "head"),
        P(None, "seq", "head"),
        P(),
        P("head", "seq"),
    )
    return jax.shard_map(
        on_device,
        mesh=mesh,
        in_specs=placed,
        out_specs=(P(None, "seq", "head"), P("head", "seq")),
        check_vma=False,
    )
```
